32 devices in a mesh: groups: 2 (over y), age: 4 (over z), span: 2 (over x), blade: 2 (over core).
Axes of the slice: x: 2, y: 2, z: 4, core: 2. Of those that a mesh axis runs over, the one named last changes fastest.
Arguments:
- surface_mu: float32 [32, 4, 64, 128], P(('groups', 'age'), 'blade', None, 'span'), parts along dimension 0, may hold values from -6 to 6
- centroid_body: float32 [3, 4, 64, 128], P(None, 'blade', None, 'span'), may hold values from -0.04 to 1.01
- area_normal: float32 [3, 4, 64, 128], P(None, 'blade', None, 'span'), may hold values from -0.12 to 0.12
- te_body: float32 [3, 4, 128], P(None, 'blade', 'span'), may hold values from -0.04 to 1.01
- wake_state: float32 [4, 4, 64, 2, 128], P(None, 'blade', ('groups', 'age'), 'span'), parts along dimension 2, may hold values from -2 to 2
- pairs: int32 [4, 64, 2, 8], P('blade', ('groups', 'age'), 'span'), parts along dimension 1, may hold values from -1 to 71, as said below
- az_index: int32 [6], P('groups'), parts along dimension 0, may hold values from 0 to 15
- free_stream: float32 [6], P('groups'), parts along dimension 0, may hold values from -3 to 3
Outputs:
- wake_final: float32 [4, 4, 64, 2, 128], P(None, 'blade', ('groups', 'age'), 'span'), parts along dimension 2
- wake_velocity: float32 [3, 4, 64, 2, 128], P(None, 'blade', ('groups', 'age'), 'span'), parts along dimension 2
The draws below stay inside these ranges and needn't reach their ends.
There are 2 independent parts, one for each index of `groups`. The reference program is written for one: setup_inputs(seed, part) draws one part's arguments, and reference() takes and returns one part's arrays. A program takes and returns all parts, laid end to end along the dimension named above; an argument that names none is the same for every part. Nothing has to cross between parts.
Inputs may be any that keep to these rules, and one draw needn't show every extreme that they name: Rows come in age blocks of 16 rows (8 tiles), spanwise panels in strips of 64. An entry v >= 0 of pairs[b, t, s, :] names tile v % 8 of age block t // 8 + v // 24 - 1 in strip s + (v // 8) % 3 - 1 of the same blade; -1 marks an empty slot. In each aligned block of 2 blades, one age block and one strip, at most 64 entries are not -1, and exactly 64 in one such block.
All inputs are finite; a program needn't handle non-finite values.
Results may differ from the reference program's by a relative error of at most 0.0003.
Values sent between devices are 32-bit elements; how exact they have to be, the bound alone decides.
A program may use at most 64 MiB of HBM per device.

```python
import math
import jax
import jax.numpy as jnp
from jax import lax

NB = 4
CH = 64
SP_DEV = 64
CB = 8
NP = 8
STEPS = 3
ROWS = 64
SPAN = 128
NAZ = 16
TILE_DEV = 8
TILES = 32
SOURCES = 512
N_AGE = 4
N_SPAN = 2
N_BLADE = 2


def draw_centroid_body(key, part):
    noise_vals = jax.random.uniform(key, (3, NB, CH, SPAN), jnp.float32, -1.0, 1.0)
    chord_pos = (jnp.arange(CH, dtype=jnp.float32) + 0.5) / CH - 0.5
    radius = 0.2 + 0.8 * (jnp.arange(SPAN, dtype=jnp.float32) + 0.5) / SPAN
    first = radius[None, None, :] + 0.01 * noise_vals[0]
    second = 0.06 * chord_pos[None, :, None] + 0.01 * noise_vals[1]
    third = 0.01 * noise_vals[2]
    return jnp.stack([first, second, third])


def draw_te_body(key, part):
    noise_vals = jax.random.uniform(key, (3, NB, SPAN), jnp.float32, -1.0, 1.0)
    radius = 0.2 + 0.8 * (jnp.arange(SPAN, dtype=jnp.float32) + 0.5) / SPAN
    first = radius[None, :] + 0.01 * noise_vals[0]
    second = -0.03 + 0.01 * noise_vals[1]
    third = 0.01 * noise_vals[2]
    return jnp.stack([first, second, third])


def draw_wake_state(key, part):
    key_jitter, key_doublet = jax.random.split(key)
    jitter = jax.random.uniform(key_jitter, (3, NB, ROWS, SPAN), jnp.float32, -1.0, 1.0)
    doublets = jnp.clip(0.7 * jax.random.normal(key_doublet, (NB, ROWS, SPAN), jnp.float32), -2.0, 2.0)
    row_ids = jnp.arange(ROWS, dtype=jnp.float32)
    blade_ids = jnp.arange(NB, dtype=jnp.float32)
    radius = 0.2 + 0.8 * (jnp.arange(SPAN, dtype=jnp.float32) + 0.5) / SPAN
    angles = 2.0 * math.pi * blade_ids[:, None, None] / NB - 0.04 * (row_ids[None, :, None] + 1.0) + 0.002 * jitter[1]
    spread = radius[None, None, :] + 0.003 * jitter[0]
    first = spread * jnp.cos(angles)
    second = spread * jnp.sin(angles)
    third = -0.004 * (row_ids[None, :, None] + 1.0) + 0.002 * jitter[2]
    sheet_grid = jnp.stack([first, second, third, doublets])
    tiled_state = sheet_grid.reshape(4, NB, ROWS // 2, 2, N_SPAN, SP_DEV).transpose(0, 1, 2, 4, 3, 5)
    return tiled_state.reshape(4, NB, ROWS // 2, N_SPAN, 2 * SP_DEV)


def draw_pairs(key, part):
    key_load, key_busy, key_rank, key_ids = jax.random.split(key, 4)
    blade_group = NB // N_BLADE
    blocks = N_BLADE * N_AGE * N_SPAN
    slot_count = blade_group * TILE_DEV * NP
    capacity = slot_count // 2
    block_loads = jax.random.randint(key_load, (blocks,), capacity // 4, capacity // 2 + 1)
    busiest = jax.random.randint(key_busy, (), 0, blocks)
    block_loads = jnp.where(jnp.arange(blocks, dtype=jnp.int32) == busiest, capacity, block_loads)
    slot_ranks = jax.vmap(lambda sub_key: jax.random.permutation(sub_key, slot_count))(jax.random.split(key_rank, blocks))
    live_mask = slot_ranks < block_loads[:, None]
    pair_ids = jax.random.randint(key_ids, (blocks, slot_count), 0, 9 * TILE_DEV)
    values = jnp.where(live_mask, pair_ids, -1)
    values = values.reshape(N_BLADE, N_AGE, N_SPAN, blade_group, TILE_DEV, NP)
    values = values.transpose(0, 3, 1, 4, 2, 5).reshape(NB, TILES, N_SPAN, NP)
    return values.astype(jnp.int32)


def levels(rng, extent, cuts, smallest, top_value):
    loudness, own = 1.0, jax.random.fold_in(rng, 6)
    for position, shards_of in cuts:
        steps = jnp.exp(jax.random.uniform(jax.random.fold_in(own, position), (shards_of,), jnp.float32, smallest / len(cuts), top_value / len(cuts)))
        loudness = loudness * jnp.repeat(steps, extent[position] // shards_of).reshape([-1 if axis == position else 1 for axis in range(len(extent))])
    return loudness


def normal_values(key, shape, scale, bound, cuts=(), kind=jnp.bfloat16):
    values = scale * jax.random.normal(key, shape, jnp.float32)
    if cuts:
        values = values * levels(key, shape, cuts, -0.22, 0.18)
    return jnp.clip(values, -bound, bound).astype(kind)


def setup_inputs(seed: int = 0, part: int = 0) -> dict:
    splits = jax.random.split(jax.random.key(seed), 9)
    part_splits = jax.random.split(jax.random.fold_in(splits[8], part), 9)
    surface_mu = normal_values(part_splits[0], (NAZ, NB, CH, SPAN), 1.0, 6.0, ((0, 4), (1, 2), (3, 2)), jnp.float32)
    centroid_body = draw_centroid_body(jax.random.fold_in(splits[8], 71), part)
    area_normal = normal_values(splits[2], (3, NB, CH, SPAN), 0.02, 0.12, ((1, 2), (3, 2)), jnp.float32)
    te_body = draw_te_body(jax.random.fold_in(splits[8], 71), part)
    wake_state = draw_wake_state(jax.random.fold_in(jax.random.fold_in(splits[8], part), 71), part)
    pairs = draw_pairs(jax.random.fold_in(jax.random.fold_in(splits[8], part), 71), part)
    az_index = jax.random.randint(part_splits[6], (STEPS,), 0, NAZ).astype(jnp.int32)
    free_stream = normal_values(part_splits[7], (3,), 0.5, 3.0, (), jnp.float32)
    return {"surface_mu": surface_mu, "centroid_body": centroid_body, "area_normal": area_normal, "te_body": te_body, "wake_state": wake_state, "pairs": pairs, "az_index": az_index, "free_stream": free_stream}


time_step = 0.05
near_core = 0.0025
far_core = 0.01
inv_four_pi = 0.25 / math.pi

def rotate(vector, cosine, sine_val):
    return jnp.stack([vector[0] * cosine - vector[1] * sine_val, vector[0] * sine_val + vector[1] * cosine, vector[2]])

def coarse_sum(values, block_size):
    shape = values.shape
    grouped = values.reshape(shape[:-2] + (shape[-2] // block_size, block_size, shape[-1] // block_size, block_size))
    return lax.optimization_barrier(jnp.sum(grouped, axis=(-3, -1)))

def far_velocity(targets, centers, moments):
    separation = targets[:, :, None] - centers[:, None, :]
    dist_sq = lax.optimization_barrier(jnp.sum(separation * separation, axis=0)) + far_core
    inverse = 1.0 / jnp.sqrt(dist_sq)
    inverse_cube = inverse * inverse * inverse
    projection = lax.optimization_barrier(jnp.sum(moments[:, None, :] * separation, axis=0))
    values = 3.0 * projection * inverse_cube * inverse * inverse * separation - moments[:, None, :] * inverse_cube
    return inv_four_pi * lax.optimization_barrier(jnp.sum(values, axis=2))

def near_velocity(targets, sources, strengths):
    separation = targets[:, :, None] - sources[:, None, :]
    dist_sq = lax.optimization_barrier(jnp.sum(separation * separation, axis=0)) + near_core
    weight = 1.0 / (dist_sq * jnp.sqrt(dist_sq))
    cross_prod = jnp.stack([strengths[1][None, :] * separation[2] - strengths[2][None, :] * separation[1], strengths[2][None, :] * separation[0] - strengths[0][None, :] * separation[2], strengths[0][None, :] * separation[1] - strengths[1][None, :] * separation[0]])
    return inv_four_pi * lax.optimization_barrier(jnp.sum(cross_prod * weight[None], axis=2))

def sheet_strength(pos_pad, mu_pad):
    pos_r = 0.5 * (pos_pad[:, :, 2:, 1:-1] - pos_pad[:, :, :-2, 1:-1])
    pos_s = 0.5 * (pos_pad[:, :, 1:-1, 2:] - pos_pad[:, :, 1:-1, :-2])
    mu_r = 0.5 * (mu_pad[:, 2:, 1:-1] - mu_pad[:, :-2, 1:-1])
    mu_s = 0.5 * (mu_pad[:, 1:-1, 2:] - mu_pad[:, 1:-1, :-2])
    return mu_s[None] * pos_r - mu_r[None] * pos_s

def tile_map(kernel, operands):
    length = jax.tree.leaves(operands)[0].shape[0]
    group_size = math.gcd(length, 8)
    shaped = jax.tree.map(lambda array: array.reshape((length // group_size, group_size) + array.shape[1:]), operands)
    result = lax.map(jax.vmap(kernel), shaped)
    return result.reshape((length,) + result.shape[2:])

def near_kernel(bundle):
    return near_velocity(bundle[0], bundle[1], bundle[2])

def to_grid(tiled_state):
    depth = tiled_state.shape[0]
    sheet_grid = tiled_state.reshape(depth, NB, TILES, N_SPAN, 2, SP_DEV)
    return sheet_grid.transpose(0, 1, 2, 4, 3, 5).reshape(depth, NB, ROWS, SPAN)

def to_tiles(sheet_grid):
    depth = sheet_grid.shape[0]
    tiled_state = sheet_grid.reshape(depth, NB, TILES, 2, N_SPAN, SP_DEV)
    return tiled_state.transpose(0, 1, 2, 4, 3, 5).reshape(depth, NB, TILES, N_SPAN, 2 * SP_DEV)

def near_field(pos_tiles, str_tiles, pairs):
    stacked = jnp.concatenate([pos_tiles, str_tiles], 0)
    padded = jnp.pad(stacked, ((0, 0), (0, 0), (TILE_DEV, TILE_DEV), (1, 1), (0, 0)))
    live_mask = (pairs >= 0).astype(jnp.float32)
    safe_ids = jnp.maximum(pairs, 0)
    tile_ids = jnp.arange(TILES, dtype=jnp.int32)[None, :, None, None]
    strip_ids = jnp.arange(N_SPAN, dtype=jnp.int32)[None, None, :, None]
    blade_ids = jnp.arange(NB, dtype=jnp.int32)[:, None, None, None]
    src_tile = (tile_ids // TILE_DEV + safe_ids // (3 * TILE_DEV)) * TILE_DEV + safe_ids % TILE_DEV
    src_strip = strip_ids + safe_ids // TILE_DEV % 3
    picked = padded[:, blade_ids, src_tile, src_strip, :]
    tile_total = NB * TILES * N_SPAN
    sources = picked[:3].reshape(3, tile_total, NP * 2 * SP_DEV).transpose(1, 0, 2)
    strengths = (picked[3:] * live_mask[None, :, :, :, :, None]).reshape(3, tile_total, NP * 2 * SP_DEV).transpose(1, 0, 2)
    targets = pos_tiles.reshape(3, tile_total, 2 * SP_DEV).transpose(1, 0, 2)
    result = tile_map(near_kernel, (targets, sources, strengths))
    return result.transpose(1, 0, 2).reshape(3, NB, TILES, N_SPAN, 2 * SP_DEV)

def reference(surface_mu, centroid_body, area_normal, te_body, wake_state, pairs, az_index, free_stream):
    state = to_grid(wake_state)
    tile_total = NB * TILES * N_SPAN
    center_body = coarse_sum(centroid_body, CB) / (CB * CB)
    blade_frac = jnp.arange(NB, dtype=jnp.float32) / NB
    velocity = jnp.zeros_like(wake_state[:3])
    for step_num in range(STEPS):
        azimuth = az_index[step_num]
        angles = 2.0 * math.pi * (azimuth.astype(jnp.float32) / NAZ + blade_frac)
        cosine = jnp.cos(angles)
        sine_val = jnp.sin(angles)
        mu_now = lax.dynamic_index_in_dim(surface_mu, azimuth, 0, keepdims=False)
        moment_body = coarse_sum(mu_now[None] * area_normal, CB)
        centers = rotate(center_body, cosine[:, None, None], sine_val[:, None, None]).reshape(3, SOURCES)
        moments = rotate(moment_body, cosine[:, None, None], sine_val[:, None, None]).reshape(3, SOURCES)
        positions = state[:3]
        doublets = state[3]
        pos_pad = jnp.pad(positions, ((0, 0), (0, 0), (1, 1), (1, 1)), mode='edge')
        mu_pad = jnp.pad(doublets, ((0, 0), (1, 1), (1, 1)))
        strength = sheet_strength(pos_pad, mu_pad)
        pos_tiles = to_tiles(positions)
        targets = pos_tiles.reshape(3, tile_total, 2 * SP_DEV).transpose(1, 0, 2)

        def far_one(target_tile):
            return far_velocity(target_tile, centers, moments)
        far_field = tile_map(far_one, targets).transpose(1, 0, 2).reshape(pos_tiles.shape)
        near_part = near_field(pos_tiles, to_tiles(strength), pairs)
        velocity = free_stream[:, None, None, None, None] + far_field + near_part
        moved = positions + time_step * to_grid(velocity)
        te_pos = rotate(te_body, cosine[:, None], sine_val[:, None])
        te_mu = mu_now[:, CH - 1, :] - mu_now[:, 0, :]
        shed_row = jnp.concatenate([te_pos, te_mu[None]], 0)
        aged = jnp.concatenate([moved, doublets[None]], 0)
        state = jnp.concatenate([shed_row[:, :, None, :], aged[:, :, :-1, :]], 2)
    return (to_tiles(state), velocity)
```

```python
import functools
import math

import jax
import jax.numpy as jnp
from jax import lax
from jax.experimental import pallas as pl
from jax.experimental.pallas import tpu as pltpu
from jax.sharding import PartitionSpec as P

CB = 8
STEP = 0.05
NEAR_CORE = 0.0025
FAR_CORE = 0.01
INV_FOUR_PI = 0.25 / math.pi
MESH = pl.DeviceIdType.MESH
HIGH = lax.Precision.HIGHEST
F32 = jnp.float32


def dot(a, b):
    return jnp.dot(a, b, preferred_element_type=F32, precision=HIGH)


def wake_kernel(
    sizes,
    az_ref, fs_ref, src_ref, tgt_ref,
    hot_ref, mu_ref, cen_ref, nrm_ref, te_ref, state_ref,
    final_ref, vel_ref,
    g1, g2, srcs, cur, moved, tile_out, shed, tail_in, side_in, far_out, near_out,
    g1_send, g1_recv, g2_send, g2_recv, a_send, a_recv, b_send, b_recv, *tables,
):
    n_age, n_span, n_blade, steps, az_dev = sizes
    entries = near_out.shape[1]
    age = lax.axis_index("age")
    span = lax.axis_index("span")
    blade = lax.axis_index("blade")
    n_plane = n_span * n_blade
    place = span * n_blade + blade
    naz = az_dev * n_age
    nb = 2 * n_blade
    first_age = age == 0
    last_age = age == n_age - 1

    for table in tables:
        table[...] = jnp.zeros_like(table)

    around = [(da, ds) for da in (-1, 0, 1) for ds in (-1, 0, 1) if (da, ds) != (0, 0)]

    def exists(da, ds):
        ok = jnp.bool_(True)
        if da < 0:
            ok = age > 0
        if da > 0:
            ok = age < n_age - 1
        if ds < 0:
            ok = jnp.logical_and(ok, span > 0)
        if ds > 0:
            ok = jnp.logical_and(ok, span < n_span - 1)
        return ok

    def spot(da, ds):
        return {"age": age + da, "span": span + ds, "blade": blade}

    def age_peer(off):
        return lax.rem(age + off, n_age)

    def plane_peer(off):
        other = lax.rem(place + off, n_plane)
        return other, {"age": age, "span": other // n_blade, "blade": lax.rem(other, n_blade)}

    diagonals = [(da, ds) for da, ds in around if da and ds]
    barrier = pltpu.get_barrier_semaphore()
    for off in range(1, n_age):
        pl.semaphore_signal(
            barrier, inc=1, device_id={"age": age_peer(off), "span": span, "blade": blade}, device_id_type=MESH
        )
    for off in range(1, n_plane):
        pl.semaphore_signal(barrier, inc=1, device_id=plane_peer(off)[1], device_id_type=MESH)
    for da, ds in diagonals:
        @pl.when(exists(da, ds))
        def _(da=da, ds=ds):
            pl.semaphore_signal(barrier, inc=1, device_id=spot(da, ds), device_id_type=MESH)

    lane8 = lax.broadcasted_iota(jnp.int32, (8, 128), 1)
    sub8 = lax.broadcasted_iota(jnp.int32, (8, 128), 0)
    low = lane8 < 64
    lane1 = lax.broadcasted_iota(jnp.int32, (1, 128), 1)
    low1 = lane1 < 64

    turn = jnp.zeros((8, 128), F32)
    for k in range(steps):
        turn = jnp.where(sub8 == k, az_ref[k].astype(F32) / naz, turn)
    frac = (blade * 2 + lane8 // 64).astype(F32) / nb
    angle = 2.0 * math.pi * (turn + frac)
    cosine = jnp.cos(angle)
    sine = jnp.sin(angle)

    def turned(k, x, y, z):
        c = cosine[k:k + 1]
        s = sine[k:k + 1]
        return x * c - y * s, x * s + y * c, z

    col = lax.broadcasted_iota(jnp.int32, (64, 128), 1)
    row = lax.broadcasted_iota(jnp.int32, (64, 128), 0)
    spread = (row // CB == col % CB).astype(F32)
    place_lane = (row == col % 64).astype(F32)
    col2 = lax.broadcasted_iota(jnp.int32, (128, 128), 1)
    row2 = lax.broadcasted_iota(jnp.int32, (128, 128), 0)
    keep = (row2 // CB == col2 // CB).astype(F32)

    def coarse(values):
        return jnp.sum(dot(values, spread) * keep, axis=0, keepdims=True)

    centers = [coarse(cen_ref[c]) * (1.0 / (CB * CB)) for c in range(3)]
    for k in range(steps):
        az = az_ref[k]
        mine = (az // az_dev == age).astype(F32)
        now = mu_ref[lax.rem(az, az_dev)]
        m = [coarse(now * nrm_ref[c]) * INV_FOUR_PI for c in range(3)]
        rows = list(turned(k, *m)) + list(turned(k, *centers))
        d0 = jnp.broadcast_to(now[63:64] - now[0:1], (8, 64))
        d1 = jnp.broadcast_to(now[127:128] - now[64:65], (8, 64))
        trail = jnp.where(low, dot(d0, place_lane), dot(d1, place_lane))[0:1]
        rows.append(trail)
        for i, value in enumerate(rows):
            g1[age, 8 * k + i:8 * k + i + 1, :] = value * mine
        g1[age, 8 * k + 7:8 * k + 8, :] = jnp.zeros((1, 128), F32)

    cur[...] = state_ref[...]
    for cb in range(8):
        tile_out[0, cb:cb + 1, :] = state_ref[cb, 7:8, :]
        tile_out[steps + 1, cb:cb + 1, :] = state_ref[cb, 0:1, :]

    peers = n_age - 1 + n_plane - 1
    for da, ds in diagonals:
        peers = peers + exists(da, ds).astype(jnp.int32)
    pl.semaphore_wait(barrier, peers)

    def send_g1(off):
        to = age_peer(off)
        return pltpu.make_async_remote_copy(
            g1.at[age], g1.at[age], g1_send.at[off], g1_recv.at[off],
            device_id={"age": to, "span": span, "blade": blade}, device_id_type=MESH)

    def recv_g1(off):
        frm = lax.rem(age - off + n_age, n_age)
        return pltpu.make_async_remote_copy(
            g1.at[age], g1.at[frm], g1_send.at[off], g1_recv.at[off],
            device_id={"age": age_peer(off), "span": span, "blade": blade}, device_id_type=MESH)

    for off in range(1, n_age):
        send_g1(off).start()

    def side_copy(k, src, ds):
        slot = 0 if ds > 0 else 1
        return pltpu.make_async_remote_copy(
            src, side_in.at[k, slot], a_send.at[k, slot], a_recv.at[k, slot],
            device_id=spot(0, ds), device_id_type=MESH)

    def tail_copy(k, src, da, ds, slot, send):
        return pltpu.make_async_remote_copy(
            src, tail_in.at[k, slot], a_send.at[k, send], a_recv.at[k, 2 + slot],
            device_id=spot(da, ds), device_id_type=MESH)

    def edge_plan(k):
        plan = []
        block = cur if k == 0 else moved.at[k - 1]
        if k < steps:
            for ds in (-1, 1):
                plan.append((exists(0, ds), exists(0, -ds), side_copy(k, block, ds)))
        plan.append((exists(1, 0), exists(-1, 0), tail_copy(k, tile_out.at[k], 1, 0, 0, 2)))
        if k == 0:
            plan.append((exists(-1, 0), exists(1, 0), tail_copy(k, tile_out.at[steps + 1], -1, 0, 3, 3)))
        elif k < steps:
            for ds in (-1, 1):
                slot = 1 if ds > 0 else 2
                plan.append((exists(1, ds), exists(-1, -ds), tail_copy(k, tile_out.at[k], 1, ds, slot, 2 + slot)))
                plan.append((
                    jnp.logical_and(first_age, exists(0, ds)), jnp.logical_and(first_age, exists(0, -ds)),
                    tail_copy(k, shed.at[k - 1], 0, ds, slot, 4 + slot)))
        return plan

    def start(plan):
        for out, _, copy in plan:
            pl.when(out)(copy.start)

    def finish(plan):
        for _, come, copy in plan:
            pl.when(come)(copy.wait_recv)
        for out, _, copy in plan:
            pl.when(out)(copy.wait_send)

    def block_plan(k):
        plan = []
        for da, ds in around:
            slot = (1 - da) * 3 + 1 - ds
            copy = pltpu.make_async_remote_copy(
                tables[k].at[pl.ds(64, 16)], tables[k].at[pl.ds(slot * 16, 16)],
                b_send.at[k, slot], b_recv.at[k, slot], device_id=spot(da, ds), device_id_type=MESH)
            plan.append((exists(da, ds), exists(-da, -ds), copy))
        return plan

    def roll64(v):
        return pltpu.roll(v, 64, 1)

    def down(v):
        return pltpu.roll(v, 1, 0)

    def aged(block, tail):
        r = roll64(block)
        first = jnp.broadcast_to(roll64(tail), (8, 128))
        return jnp.where(low, jnp.where(sub8 == 0, first, down(r)), r)

    def strengths(k):
        for b in range(2):
            diff = []
            for c in range(4):
                cb = 2 * c + b
                v = cur[cb]
                r = roll64(v)
                own_pos = c < 3
                above_edge = v[0:1] if own_pos else jnp.zeros((1, 128), F32)
                below_edge = v[7:8] if own_pos else jnp.zeros((1, 128), F32)
                tail = tail_in[k, 0, cb:cb + 1, :]
                if k == 0:
                    up_row = jnp.where(first_age, above_edge, roll64(tail))
                    head = tail_in[k, 3, cb:cb + 1, :]
                    down_row = jnp.where(last_age, below_edge, roll64(head))
                else:
                    up_row = jnp.where(first_age, above_edge, tail)
                    down_row = jnp.where(last_age, below_edge, moved[k - 1, cb, 7:8, :])
                before = jnp.where(low, jnp.where(sub8 == 0, jnp.broadcast_to(up_row, (8, 128)), down(r)), r)
                after = jnp.where(
                    low, r, jnp.where(sub8 == 7, jnp.broadcast_to(down_row, (8, 128)), pltpu.roll(r, 7, 0)))
                edge = v if own_pos else jnp.zeros((8, 128), F32)
                left, right = side_in[k, 0, cb], side_in[k, 1, cb]
                if k > 0:
                    left = aged(left, tail_in[k, 1, cb:cb + 1, :])
                    right = aged(right, tail_in[k, 2, cb:cb + 1, :])
                left = jnp.where(span == 0, edge, pltpu.roll(left, 65, 1))
                right = jnp.where(span == n_span - 1, edge, pltpu.roll(right, 63, 1))
                minus = jnp.where(lane8 % 64 == 0, left, pltpu.roll(v, 1, 1))
                plus = jnp.where(lane8 % 64 == 63, right, pltpu.roll(v, 127, 1))
                diff.append((0.5 * (after - before), 0.5 * (plus - minus)))
                if own_pos:
                    for t in range(8):
                        tables[k][64 + b * 8 + t, c:c + 1, :] = v[t:t + 1]
            mu_r, mu_s = diff[3]
            for c in range(3):
                value = (mu_s * diff[c][0] - mu_r * diff[c][1]) * INV_FOUR_PI
                for t in range(8):
                    tables[k][64 + b * 8 + t, 3 + c:4 + c, :] = value[t:t + 1]

    groups = srcs.shape[1] // 8

    def fill_sources(k):
        for p in range(n_plane):
            cols = jnp.transpose(g2[p, 8 * k:8 * k + 8, :])
            for i in range(6):
                srcs[i, 128 * p:128 * p + 128, :] = jnp.broadcast_to(cols[:, i:i + 1], (128, 128))

    def far(t0):
        def per_blade(b, carry):
            goal = [
                [jnp.broadcast_to(cur[2 * c + b, t0 + i:t0 + i + 1, :], (8, 128)) for c in range(3)]
                for i in range(4)
            ]

            def body(g, acc):
                at = pl.ds(pl.multiple_of(g * 8, 8), 8)
                cx, cy, cz = srcs[3, at, :], srcs[4, at, :], srcs[5, at, :]
                mx, my, mz = srcs[0, at, :], srcs[1, at, :], srcs[2, at, :]
                out = []
                for i in range(4):
                    dx, dy, dz = goal[i][0] - cx, goal[i][1] - cy, goal[i][2] - cz
                    r = lax.rsqrt(dx * dx + dy * dy + (dz * dz + FAR_CORE))
                    r2 = r * r
                    r3 = r2 * r
                    t = (mx * dx + my * dy + mz * dz) * (3.0 * r2)
                    out.append(acc[3 * i] + r3 * (t * dx - mx))
                    out.append(acc[3 * i + 1] + r3 * (t * dy - my))
                    out.append(acc[3 * i + 2] + r3 * (t * dz - mz))
                return tuple(out)

            acc = lax.fori_loop(0, groups, body, tuple(jnp.zeros((8, 128), F32) for _ in range(12)))
            for i in range(4):
                for c in range(3):
                    far_out[2 * c + b, t0 + i:t0 + i + 1, :] = jnp.sum(acc[3 * i + c], axis=0, keepdims=True)
            return carry

        lax.fori_loop(0, 2, per_blade, 0)

    def near(k):
        def body(e, carry):
            s = src_ref[e]
            t = tgt_ref[e]
            cols = jnp.transpose(tables[k][s])
            goal_tile = tables[k][64 + t]
            goal = [jnp.broadcast_to(goal_tile[c:c + 1], (8, 128)) for c in range(3)]
            acc = [jnp.zeros((8, 128), F32) for _ in range(3)]
            for g in range(16):
                part = cols[8 * g:8 * g + 8, :]
                px, py, pz, sx, sy, sz = [jnp.broadcast_to(part[:, i:i + 1], (8, 128)) for i in range(6)]
                dx, dy, dz = goal[0] - px, goal[1] - py, goal[2] - pz
                r = lax.rsqrt(dx * dx + dy * dy + (dz * dz + NEAR_CORE))
                w = r * r * r
                acc[0] += w * (sy * dz - sz * dy)
                acc[1] += w * (sz * dx - sx * dz)
                acc[2] += w * (sx * dy - sy * dx)
            for c in range(3):
                near_out[c, pl.ds(e, 1), :] = jnp.sum(acc[c], axis=0, keepdims=True)
            return carry

        lax.fori_loop(0, entries, body, 0)

    plan = edge_plan(0)
    start(plan)
    finish(plan)
    strengths(0)
    blocks = block_plan(0)
    start(blocks)

    for off in range(1, n_age):
        recv_g1(off).wait_recv()
    total = g1[0]
    for i in range(1, n_age):
        total = total + g1[i]
    g2[place] = total

    def send_g2(off):
        return pltpu.make_async_remote_copy(
            g2.at[place], g2.at[place], g2_send.at[off], g2_recv.at[off],
            device_id=plane_peer(off)[1], device_id_type=MESH)

    def recv_g2(off):
        frm = lax.rem(place - off + n_plane, n_plane)
        return pltpu.make_async_remote_copy(
            g2.at[place], g2.at[frm], g2_send.at[off], g2_recv.at[off],
            device_id=plane_peer(off)[1], device_id_type=MESH)

    for off in range(1, n_plane):
        send_g2(off).start()

    for k in range(steps):
        te = turned(k, te_ref[0:1], te_ref[1:2], te_ref[2:3])
        lines = list(te) + [total[8 * k + 6:8 * k + 7]]
        for c in range(4):
            flipped = roll64(lines[c])
            beyond = (lines[c], flipped) if c < 3 else (jnp.zeros((1, 128), F32),) * 2
            shed[k, 2 * c:2 * c + 1, :] = jnp.where(low1, beyond[0], flipped)
            shed[k, 2 * c + 1:2 * c + 2, :] = jnp.where(low1, beyond[1], lines[c])

    for off in range(1, n_plane):
        recv_g2(off).wait_recv()
    for off in range(1, n_age):
        send_g1(off).wait_send()
    for off in range(1, n_plane):
        send_g2(off).wait_send()

    def incoming(k, cb):
        return jnp.where(first_age, shed[k - 1, cb:cb + 1, :], tail_in[k, 0, cb:cb + 1, :])

    for k in range(steps):
        fill_sources(k)
        far(4)
        if k > 0:
            finish(plan)
            for cb in range(8):
                cur[cb] = aged(moved[k - 1, cb], incoming(k, cb))
            strengths(k)
            blocks = block_plan(k)
            start(blocks)
        far(0)
        finish(blocks)
        near(k)
        hot = hot_ref[...]
        for c in range(3):
            close = dot(hot, near_out[c])
            for b in range(2):
                v = fs_ref[c] + far_out[2 * c + b] + close[8 * b:8 * b + 8]
                if k == steps - 1:
                    vel_ref[2 * c + b] = v
                moved[k, 2 * c + b] = cur[2 * c + b] + STEP * v
        for b in range(2):
            moved[k, 6 + b] = cur[6 + b]
        for cb in range(8):
            tile_out[k + 1, cb:cb + 1, :] = moved[k, cb, 7:8, :]
        plan = edge_plan(k + 1)
        start(plan)
        if k < steps - 1:
            for cb in range(8):
                cur[cb] = aged(moved[k, cb], shed[k, cb:cb + 1, :])
    finish(plan)
    for cb in range(8):
        final_ref[cb] = aged(moved[steps - 1, cb], incoming(steps, cb))


def on_device(
    surface_mu, centroid_body, area_normal, te_body, wake_state, pairs, az_index, free_stream
):
    az_dev = surface_mu.shape[0]
    blades, tiles = wake_state.shape[1:3]
    steps = az_index.shape[0]
    slots = pairs.shape[3]
    n_age, n_span, n_blade = (lax.axis_size(a) for a in ("age", "span", "blade"))
    n_plane = n_span * n_blade
    count = blades * tiles * slots
    entries = count // 2

    ids = pairs.reshape(count)
    live = ids >= 0
    order = jnp.arange(count, dtype=jnp.int32)
    rank = jnp.sum((live[None, :] & (order[None, :] < order[:, None])).astype(jnp.int32), axis=1)
    chosen = live[None, :] & (rank[None, :] == jnp.arange(entries, dtype=jnp.int32)[:, None])
    place = (ids // 8) * (blades * tiles) + order // (tiles * slots) * tiles + ids % 8
    empty = 9 * blades * tiles
    src = empty + jnp.sum(jnp.where(chosen, place[None, :] - empty, 0), axis=1)
    tgt = jnp.sum(jnp.where(chosen, order[None, :] // slots, 0), axis=1)
    hot = (tgt[None, :] == jnp.arange(blades * tiles, dtype=jnp.int32)[:, None]).astype(F32)

    vm = pl.BlockSpec(memory_space=pltpu.VMEM)
    sm = pl.BlockSpec(memory_space=pltpu.SMEM)
    dma = pltpu.SemaphoreType.DMA
    final, vel = pl.pallas_call(
        functools.partial(wake_kernel, (n_age, n_span, n_blade, steps, az_dev)),
        out_shape=(
            jax.ShapeDtypeStruct((8, 8, 128), F32),
            jax.ShapeDtypeStruct((6, 8, 128), F32),
        ),
        in_specs=[sm] * 4 + [vm] * 6,
        out_specs=(vm, vm),
        scratch_shapes=[
            pltpu.VMEM((n_age, 8 * steps, 128), F32),
            pltpu.VMEM((n_plane, 8 * steps, 128), F32),
            pltpu.VMEM((6, 128 * n_plane, 128), F32),
            pltpu.VMEM((8, 8, 128), F32),
            pltpu.VMEM((steps, 8, 8, 128), F32),
            pltpu.VMEM((steps + 2, 8, 128), F32),
            pltpu.VMEM((steps, 8, 128), F32),
            pltpu.VMEM((steps + 1, 4, 8, 128), F32),
            pltpu.VMEM((steps, 2, 8, 8, 128), F32),
            pltpu.VMEM((6, 8, 128), F32),
            pltpu.VMEM((3, entries, 128), F32),
            dma((n_age,)),
            dma((n_age,)),
            dma((n_plane,)),
            dma((n_plane,)),
            dma((steps + 1, 7)),
            dma((steps + 1, 6)),
            dma((steps, 9)),
            dma((steps, 9)),
        ] + [pltpu.VMEM((empty + 1, 8, 128), F32)] * steps,
        compiler_params=pltpu.CompilerParams(
            collective_id=0, has_side_effects=True, vmem_limit_bytes=40 * 1024 * 1024
        ),
    )(
        az_index,
        free_stream,
        src,
        tgt,
        hot,
        surface_mu.reshape(az_dev, 128, 64),
        centroid_body.reshape(3, 128, 64),
        area_normal.reshape(3, 128, 64),
        te_body.reshape(3, 128),
        wake_state.reshape(8, 8, 128),
    )
    return (
        final.reshape(4, blades, tiles, 1, 128),
        vel.reshape(3, blades, tiles, 1, 128),
    )


def solution(mesh):
    in_specs = (
        P(("groups", "age"), "blade", None, "span"),
        P(None, "blade", None, "span"),
        P(None, "blade", None, "span"),
        P(None, "blade", "span"),
        P(None, "blade", ("groups", "age"), "span", None),
        P("blade", ("groups", "age"), "span", None),
        P("groups"),
        P("groups"),
    )
    out_specs = (
        P(None, "blade", ("groups", "age"), "span", None),
        P(None, "blade", ("groups", "age"), "span", None),
    )
    return jax.shard_map(
        on_device, mesh=mesh, in_specs=in_specs, out_specs=out_specs, check_vma=False
    )
```

```python
import functools
import math

import jax
import jax.numpy as jnp
from jax import lax
from jax.experimental import pallas as pl
from jax.experimental.pallas import tpu as pltpu
from jax.sharding import PartitionSpec as P

CB = 8
STEP = 0.05
NEAR_CORE = 0.0025
FAR_CORE = 0.01
INV_FOUR_PI = 0.25 / math.pi
MESH = pl.DeviceIdType.MESH
HIGH = lax.Precision.HIGHEST
F32 = jnp.float32


def dot(a, b):
    return jnp.dot(a, b, preferred_element_type=F32, precision=HIGH)


def wake_kernel(
    sizes,
    az_ref, fs_ref, src_ref, tgt_ref,
    hot_ref, mu_ref, cen_ref, nrm_ref, te_ref, state_ref,
    final_ref, vel_ref,
    g1, g2, srcs, cur, moved, tile_out, shed, tail_in, side_in, far_out, near_out, goals,
    g1_send, g1_recv, g2_send, g2_recv, a_send, a_recv, b_send, b_recv, *tables,
):
    n_age, n_span, n_blade, steps, az_dev = sizes
    entries = near_out.shape[1]
    age = lax.axis_index("age")
    span = lax.axis_index("span")
    blade = lax.axis_index("blade")
    n_plane = n_span * n_blade
    place = span * n_blade + blade
    naz = az_dev * n_age
    nb = 2 * n_blade
    first_age = age == 0
    last_age = age == n_age - 1

    for table in tables:
        table[...] = jnp.zeros_like(table)

    around = [(da, ds) for da in (-1, 0, 1) for ds in (-1, 0, 1) if (da, ds) != (0, 0)]

    def exists(da, ds):
        ok = jnp.bool_(True)
        if da < 0:
            ok = age > 0
        if da > 0:
            ok = age < n_age - 1
        if ds < 0:
            ok = jnp.logical_and(ok, span > 0)
        if ds > 0:
            ok = jnp.logical_and(ok, span < n_span - 1)
        return ok

    def spot(da, ds):
        return {"age": age + da, "span": span + ds, "blade": blade}

    def age_peer(off):
        return lax.rem(age + off, n_age)

    def plane_peer(off):
        other = lax.rem(place + off, n_plane)
        return other, {"age": age, "span": other // n_blade, "blade": lax.rem(other, n_blade)}

    diagonals = [(da, ds) for da, ds in around if da and ds]
    barrier = pltpu.get_barrier_semaphore()
    for off in range(1, n_age):
        pl.semaphore_signal(
            barrier, inc=1, device_id={"age": age_peer(off), "span": span, "blade": blade}, device_id_type=MESH
        )
    for off in range(1, n_plane):
        pl.semaphore_signal(barrier, inc=1, device_id=plane_peer(off)[1], device_id_type=MESH)
    for da, ds in diagonals:
        @pl.when(exists(da, ds))
        def _(da=da, ds=ds):
            pl.semaphore_signal(barrier, inc=1, device_id=spot(da, ds), device_id_type=MESH)

    lane8 = lax.broadcasted_iota(jnp.int32, (8, 128), 1)
    sub8 = lax.broadcasted_iota(jnp.int32, (8, 128), 0)
    low = lane8 < 64
    lane1 = lax.broadcasted_iota(jnp.int32, (1, 128), 1)
    low1 = lane1 < 64

    turn = jnp.zeros((8, 128), F32)
    for k in range(steps):
        turn = jnp.where(sub8 == k, az_ref[k].astype(F32) / naz, turn)
    frac = (blade * 2 + lane8 // 64).astype(F32) / nb
    angle = 2.0 * math.pi * (turn + frac)
    cosine = jnp.cos(angle)
    sine = jnp.sin(angle)

    def turned(k, x, y, z):
        c = cosine[k:k + 1]
        s = sine[k:k + 1]
        return x * c - y * s, x * s + y * c, z

    col = lax.broadcasted_iota(jnp.int32, (64, 128), 1)
    row = lax.broadcasted_iota(jnp.int32, (64, 128), 0)
    spread = (row // CB == col % CB).astype(F32)
    place_lane = (row == col % 64).astype(F32)
    col2 = lax.broadcasted_iota(jnp.int32, (128, 128), 1)
    row2 = lax.broadcasted_iota(jnp.int32, (128, 128), 0)
    keep = (row2 // CB == col2 // CB).astype(F32)

    def coarse(values):
        return jnp.sum(dot(values, spread) * keep, axis=0, keepdims=True)

    centers = [coarse(cen_ref[c]) * (1.0 / (CB * CB)) for c in range(3)]
    for k in range(steps):
        az = az_ref[k]
        mine = (az // az_dev == age).astype(F32)
        now = mu_ref[lax.rem(az, az_dev)]
        m = [coarse(now * nrm_ref[c]) * INV_FOUR_PI for c in range(3)]
        rows = list(turned(k, *m)) + list(turned(k, *centers))
        d0 = jnp.broadcast_to(now[63:64] - now[0:1], (8, 64))
        d1 = jnp.broadcast_to(now[127:128] - now[64:65], (8, 64))
        trail = jnp.where(low, dot(d0, place_lane), dot(d1, place_lane))[0:1]
        rows.append(trail)
        for i, value in enumerate(rows):
            g1[age, 8 * k + i:8 * k + i + 1, :] = value * mine
        g1[age, 8 * k + 7:8 * k + 8, :] = jnp.zeros((1, 128), F32)

    cur[...] = state_ref[...]
    for cb in range(8):
        tile_out[0, cb:cb + 1, :] = state_ref[cb, 7:8, :]
        tile_out[steps + 1, cb:cb + 1, :] = state_ref[cb, 0:1, :]

    peers = n_age - 1 + n_plane - 1
    for da, ds in diagonals:
        peers = peers + exists(da, ds).astype(jnp.int32)
    pl.semaphore_wait(barrier, peers)

    def send_g1(off):
        to = age_peer(off)
        return pltpu.make_async_remote_copy(
            g1.at[age], g1.at[age], g1_send.at[off], g1_recv.at[off],
            device_id={"age": to, "span": span, "blade": blade}, device_id_type=MESH)

    def recv_g1(off):
        frm = lax.rem(age - off + n_age, n_age)
        return pltpu.make_async_remote_copy(
            g1.at[age], g1.at[frm], g1_send.at[off], g1_recv.at[off],
            device_id={"age": age_peer(off), "span": span, "blade": blade}, device_id_type=MESH)

    for off in range(1, n_age):
        send_g1(off).start()

    def side_copy(k, src, ds):
        slot = 0 if ds > 0 else 1
        return pltpu.make_async_remote_copy(
            src, side_in.at[k, slot], a_send.at[k, slot], a_recv.at[k, slot],
            device_id=spot(0, ds), device_id_type=MESH)

    def tail_copy(k, src, da, ds, slot, send):
        return pltpu.make_async_remote_copy(
            src, tail_in.at[k, slot], a_send.at[k, send], a_recv.at[k, 2 + slot],
            device_id=spot(da, ds), device_id_type=MESH)

    def edge_plan(k):
        plan = []
        block = cur if k == 0 else moved.at[k - 1]
        if k < steps:
            for ds in (-1, 1):
                plan.append((exists(0, ds), exists(0, -ds), side_copy(k, block, ds)))
        plan.append((exists(1, 0), exists(-1, 0), tail_copy(k, tile_out.at[k], 1, 0, 0, 2)))
        if k == 0:
            plan.append((exists(-1, 0), exists(1, 0), tail_copy(k, tile_out.at[steps + 1], -1, 0, 3, 3)))
        elif k < steps:
            for ds in (-1, 1):
                slot = 1 if ds > 0 else 2
                plan.append((exists(1, ds), exists(-1, -ds), tail_copy(k, tile_out.at[k], 1, ds, slot, 2 + slot)))
                plan.append((
                    jnp.logical_and(first_age, exists(0, ds)), jnp.logical_and(first_age, exists(0, -ds)),
                    tail_copy(k, shed.at[k - 1], 0, ds, slot, 4 + slot)))
        return plan

    def start(plan):
        for out, _, copy in plan:
            pl.when(out)(copy.start)

    def finish(plan):
        for _, come, copy in plan:
            pl.when(come)(copy.wait_recv)
        for out, _, copy in plan:
            pl.when(out)(copy.wait_send)

    def block_plan(k):
        plan = []
        for da, ds in around:
            slot = (1 - da) * 3 + 1 - ds
            copy = pltpu.make_async_remote_copy(
                tables[k].at[pl.ds(64, 16)], tables[k].at[pl.ds(slot * 16, 16)],
                b_send.at[k, slot], b_recv.at[k, slot], device_id=spot(da, ds), device_id_type=MESH)
            plan.append((exists(da, ds), exists(-da, -ds), copy))
        return plan

    def roll64(v):
        return pltpu.roll(v, 64, 1)

    def down(v):
        return pltpu.roll(v, 1, 0)

    def aged(block, tail):
        r = roll64(block)
        first = jnp.broadcast_to(roll64(tail), (8, 128))
        return jnp.where(low, jnp.where(sub8 == 0, first, down(r)), r)

    def strengths(k):
        for b in range(2):
            diff = []
            for c in range(4):
                cb = 2 * c + b
                v = cur[cb]
                r = roll64(v)
                own_pos = c < 3
                above_edge = v[0:1] if own_pos else jnp.zeros((1, 128), F32)
                below_edge = v[7:8] if own_pos else jnp.zeros((1, 128), F32)
                tail = tail_in[k, 0, cb:cb + 1, :]
                if k == 0:
                    up_row = jnp.where(first_age, above_edge, roll64(tail))
                    head = tail_in[k, 3, cb:cb + 1, :]
                    down_row = jnp.where(last_age, below_edge, roll64(head))
                else:
                    up_row = jnp.where(first_age, above_edge, tail)
                    down_row = jnp.where(last_age, below_edge, moved[k - 1, cb, 7:8, :])
                before = jnp.where(low, jnp.where(sub8 == 0, jnp.broadcast_to(up_row, (8, 128)), down(r)), r)
                after = jnp.where(
                    low, r, jnp.where(sub8 == 7, jnp.broadcast_to(down_row, (8, 128)), pltpu.roll(r, 7, 0)))
                edge = v if own_pos else jnp.zeros((8, 128), F32)
                left, right = side_in[k, 0, cb], side_in[k, 1, cb]
                if k > 0:
                    left = aged(left, tail_in[k, 1, cb:cb + 1, :])
                    right = aged(right, tail_in[k, 2, cb:cb + 1, :])
                left = jnp.where(span == 0, edge, pltpu.roll(left, 65, 1))
                right = jnp.where(span == n_span - 1, edge, pltpu.roll(right, 63, 1))
                minus = jnp.where(lane8 % 64 == 0, left, pltpu.roll(v, 1, 1))
                plus = jnp.where(lane8 % 64 == 63, right, pltpu.roll(v, 127, 1))
                diff.append((0.5 * (after - before), 0.5 * (plus - minus)))
                if own_pos:
                    for t in range(8):
                        tables[k][64 + b * 8 + t, c:c + 1, :] = v[t:t + 1]
            mu_r, mu_s = diff[3]
            for c in range(3):
                value = (mu_s * diff[c][0] - mu_r * diff[c][1]) * INV_FOUR_PI
                for t in range(8):
                    tables[k][64 + b * 8 + t, 3 + c:4 + c, :] = value[t:t + 1]

    groups = srcs.shape[1] // 8

    def fill_sources(k):
        for p in range(n_plane):
            cols = jnp.transpose(g2[p, 8 * k:8 * k + 8, :])
            for i in range(6):
                srcs[i, 128 * p:128 * p + 128, :] = jnp.broadcast_to(cols[:, i:i + 1], (128, 128))

    def far(t0):
        def per_blade(b, carry):
            goal = [
                [jnp.broadcast_to(cur[2 * c + b, t0 + i:t0 + i + 1, :], (8, 128)) for c in range(3)]
                for i in range(4)
            ]

            def body(g, acc):
                at = pl.ds(pl.multiple_of(g * 8, 8), 8)
                cx, cy, cz = srcs[3, at, :], srcs[4, at, :], srcs[5, at, :]
                mx, my, mz = srcs[0, at, :], srcs[1, at, :], srcs[2, at, :]
                out = []
                for i in range(4):
                    dx, dy, dz = goal[i][0] - cx, goal[i][1] - cy, goal[i][2] - cz
                    r = lax.rsqrt(dx * dx + dy * dy + (dz * dz + FAR_CORE))
                    r2 = r * r
                    r3 = r2 * r
                    t = (mx * dx + my * dy + mz * dz) * (3.0 * r2)
                    out.append(acc[3 * i] + r3 * (t * dx - mx))
                    out.append(acc[3 * i + 1] + r3 * (t * dy - my))
                    out.append(acc[3 * i + 2] + r3 * (t * dz - mz))
                return tuple(out)

            acc = lax.fori_loop(0, groups, body, tuple(jnp.zeros((8, 128), F32) for _ in range(12)))
            for i in range(4):
                for c in range(3):
                    far_out[2 * c + b, t0 + i:t0 + i + 1, :] = jnp.sum(acc[3 * i + c], axis=0, keepdims=True)
            return carry

        lax.fori_loop(0, 2, per_blade, 0)

    def fill_goals(k):
        def body(t, carry):
            cols = jnp.transpose(tables[k][64 + t])
            for c in range(3):
                for g in range(16):
                    goals[c, 16 * t + g] = jnp.broadcast_to(cols[8 * g:8 * g + 8, c:c + 1], (8, 128))
            return carry

        lax.fori_loop(0, 16, body, 0, unroll=4)

    def near(k):
        def body(e, carry):
            s = src_ref[e]
            base = tgt_ref[e] * 16
            tile = tables[k][s]
            p = [tile[c:c + 1] for c in range(3)]
            st = [tile[3 + c:4 + c] for c in range(3)]
            wide = [jnp.broadcast_to(v, (8, 128)) for v in p]
            parts = []
            for g in range(16):
                dx, dy, dz = [goals[c, base + g] - wide[c] for c in range(3)]
                r = lax.rsqrt(dx * dx + dy * dy + (dz * dz + NEAR_CORE))
                parts.append(r * r * r)
            weight = jnp.concatenate(parts, axis=0)
            qx, qy, qz = [p[c] - goals[c, base][0:1] for c in range(3)]
            rows = st + [
                st[1] * qz - st[2] * qy, st[2] * qx - st[0] * qz, st[0] * qy - st[1] * qx,
                jnp.zeros((2, 128), F32)]
            def split(v):
                hi = v.astype(jnp.bfloat16)
                rest = v - hi.astype(F32)
                mid = rest.astype(jnp.bfloat16)
                return hi, mid, (rest - mid.astype(F32)).astype(jnp.bfloat16)

            stack = jnp.concatenate([v.astype(F32) for v in split(jnp.concatenate(rows, axis=0))], axis=0)
            stack = stack.astype(jnp.bfloat16)
            full = sum(
                lax.dot_general(stack, v, (((1,), (1,)), ((), ())), preferred_element_type=F32)
                for v in split(weight))
            out = full[0:8] + full[8:16] + full[16:24]
            for i in range(6):
                near_out[i, pl.ds(e, 1), :] = out[i:i + 1]
            return carry

        lax.fori_loop(0, entries, body, 0, unroll=8)

    def close(k):
        hot = hot_ref[...]
        sums = [dot(hot, near_out[i]) for i in range(6)]
        result = [[None, None] for _ in range(3)]
        for b in range(2):
            a = [sums[i][8 * b:8 * b + 8] for i in range(6)]
            x = [cur[2 * c + b] - cur[2 * c + b, :, 0:1] for c in range(3)]
            result[0][b] = a[1] * x[2] - a[2] * x[1] - a[3]
            result[1][b] = a[2] * x[0] - a[0] * x[2] - a[4]
            result[2][b] = a[0] * x[1] - a[1] * x[0] - a[5]
        return result

    plan = edge_plan(0)
    start(plan)
    finish(plan)
    strengths(0)
    blocks = block_plan(0)
    start(blocks)

    for off in range(1, n_age):
        recv_g1(off).wait_recv()
    total = g1[0]
    for i in range(1, n_age):
        total = total + g1[i]
    g2[place] = total

    def send_g2(off):
        return pltpu.make_async_remote_copy(
            g2.at[place], g2.at[place], g2_send.at[off], g2_recv.at[off],
            device_id=plane_peer(off)[1], device_id_type=MESH)

    def recv_g2(off):
        frm = lax.rem(place - off + n_plane, n_plane)
        return pltpu.make_async_remote_copy(
            g2.at[place], g2.at[frm], g2_send.at[off], g2_recv.at[off],
            device_id=plane_peer(off)[1], device_id_type=MESH)

    for off in range(1, n_plane):
        send_g2(off).start()

    for k in range(steps):
        te = turned(k, te_ref[0:1], te_ref[1:2], te_ref[2:3])
        lines = list(te) + [total[8 * k + 6:8 * k + 7]]
        for c in range(4):
            flipped = roll64(lines[c])
            beyond = (lines[c], flipped) if c < 3 else (jnp.zeros((1, 128), F32),) * 2
            shed[k, 2 * c:2 * c + 1, :] = jnp.where(low1, beyond[0], flipped)
            shed[k, 2 * c + 1:2 * c + 2, :] = jnp.where(low1, beyond[1], lines[c])

    for off in range(1, n_plane):
        recv_g2(off).wait_recv()
    for off in range(1, n_age):
        send_g1(off).wait_send()
    for off in range(1, n_plane):
        send_g2(off).wait_send()

    def incoming(k, cb):
        return jnp.where(first_age, shed[k - 1, cb:cb + 1, :], tail_in[k, 0, cb:cb + 1, :])

    for k in range(steps):
        fill_sources(k)
        far(4)
        if k > 0:
            finish(plan)
            for cb in range(8):
                cur[cb] = aged(moved[k - 1, cb], incoming(k, cb))
            strengths(k)
            blocks = block_plan(k)
            start(blocks)
        far(0)
        fill_goals(k)
        finish(blocks)
        near(k)
        beside = close(k)
        for c in range(3):
            for b in range(2):
                v = fs_ref[c] + far_out[2 * c + b] + beside[c][b]
                if k == steps - 1:
                    vel_ref[2 * c + b] = v
                moved[k, 2 * c + b] = cur[2 * c + b] + STEP * v
        for b in range(2):
            moved[k, 6 + b] = cur[6 + b]
        for cb in range(8):
            tile_out[k + 1, cb:cb + 1, :] = moved[k, cb, 7:8, :]
        plan = edge_plan(k + 1)
        start(plan)
        if k < steps - 1:
            for cb in range(8):
                cur[cb] = aged(moved[k, cb], shed[k, cb:cb + 1, :])
    finish(plan)
    for cb in range(8):
        final_ref[cb] = aged(moved[steps - 1, cb], incoming(steps, cb))


def on_device(
    surface_mu, centroid_body, area_normal, te_body, wake_state, pairs, az_index, free_stream
):
    az_dev = surface_mu.shape[0]
    blades, tiles = wake_state.shape[1:3]
    steps = az_index.shape[0]
    slots = pairs.shape[3]
    n_age, n_span, n_blade = (lax.axis_size(a) for a in ("age", "span", "blade"))
    n_plane = n_span * n_blade
    count = blades * tiles * slots
    entries = count // 2

    ids = pairs.reshape(count)
    live = ids >= 0
    order = jnp.arange(count, dtype=jnp.int32)
    rank = jnp.sum((live[None, :] & (order[None, :] < order[:, None])).astype(jnp.int32), axis=1)
    chosen = live[None, :] & (rank[None, :] == jnp.arange(entries, dtype=jnp.int32)[:, None])
    place = (ids // 8) * (blades * tiles) + order // (tiles * slots) * tiles + ids % 8
    empty = 9 * blades * tiles
    src = empty + jnp.sum(jnp.where(chosen, place[None, :] - empty, 0), axis=1)
    tgt = jnp.sum(jnp.where(chosen, order[None, :] // slots, 0), axis=1)
    hot = (tgt[None, :] == jnp.arange(blades * tiles, dtype=jnp.int32)[:, None]).astype(F32)

    vm = pl.BlockSpec(memory_space=pltpu.VMEM)
    sm = pl.BlockSpec(memory_space=pltpu.SMEM)
    dma = pltpu.SemaphoreType.DMA
    final, vel = pl.pallas_call(
        functools.partial(wake_kernel, (n_age, n_span, n_blade, steps, az_dev)),
        out_shape=(
            jax.ShapeDtypeStruct((8, 8, 128), F32),
            jax.ShapeDtypeStruct((6, 8, 128), F32),
        ),
        in_specs=[sm] * 4 + [vm] * 6,
        out_specs=(vm, vm),
        scratch_shapes=[
            pltpu.VMEM((n_age, 8 * steps, 128), F32),
            pltpu.VMEM((n_plane, 8 * steps, 128), F32),
            pltpu.VMEM((6, 128 * n_plane, 128), F32),
            pltpu.VMEM((8, 8, 128), F32),
            pltpu.VMEM((steps, 8, 8, 128), F32),
            pltpu.VMEM((steps + 2, 8, 128), F32),
            pltpu.VMEM((steps, 8, 128), F32),
            pltpu.VMEM((steps + 1, 4, 8, 128), F32),
            pltpu.VMEM((steps, 2, 8, 8, 128), F32),
            pltpu.VMEM((6, 8, 128), F32),
            pltpu.VMEM((6, entries, 128), F32),
            pltpu.VMEM((3, 16 * 16, 8, 128), F32),
            dma((n_age,)),
            dma((n_age,)),
            dma((n_plane,)),
            dma((n_plane,)),
            dma((steps + 1, 7)),
            dma((steps + 1, 6)),
            dma((steps, 9)),
            dma((steps, 9)),
        ] + [pltpu.VMEM((empty + 1, 8, 128), F32)] * steps,
        compiler_params=pltpu.CompilerParams(
            collective_id=0, has_side_effects=True, vmem_limit_bytes=40 * 1024 * 1024
        ),
    )(
        az_index,
        free_stream,
        src,
        tgt,
        hot,
        surface_mu.reshape(az_dev, 128, 64),
        centroid_body.reshape(3, 128, 64),
        area_normal.reshape(3, 128, 64),
        te_body.reshape(3, 128),
        wake_state.reshape(8, 8, 128),
    )
    return (
        final.reshape(4, blades, tiles, 1, 128),
        vel.reshape(3, blades, tiles, 1, 128),
    )


def solution(mesh):
    in_specs = (
        P(("groups", "age"), "blade", None, "span"),
        P(None, "blade", None, "span"),
        P(None, "blade", None, "span"),
        P(None, "blade", "span"),
        P(None, "blade", ("groups", "age"), "span", None),
        P("blade", ("groups", "age"), "span", None),
        P("groups"),
        P("groups"),
    )
    out_specs = (
        P(None, "blade", ("groups", "age"), "span", None),
        P(None, "blade", ("groups", "age"), "span", None),
    )
    return jax.shard_map(
        on_device, mesh=mesh, in_specs=in_specs, out_specs=out_specs, check_vma=False
    )
```
